32 devices in a mesh: grp: 1, lat: 1, lon: 32 (over z, y, x, core).
Axes of the slice: x: 2, y: 2, z: 4, core: 2. Of those that a mesh axis runs over, the one named last changes fastest.
Arguments:
- state: float32 [5, 128, 32, 128], P(None, 'lon', 'lat', 'grp'), may hold values from -5 to 5
- tracers: float32 [12, 32, 128, 128], P(None, 'lat', ('grp', 'lon')), may hold values from 0.1 to 1.5
- coupling: float32 [5, 5], replicated, may hold values from -0.8 to 0.8
- rates: float32 [24], replicated, may hold values from 0.05 to 0.5
- pairs: int32 [24, 3], replicated, may hold values from 0 to 11
- heat_map: int32 [12], replicated, may hold values from 0 to 3
- heat_coef: float32 [4], replicated, may hold values from 0.5 to 2
Outputs:
- state_out: float32 [5, 128, 32, 128], P(None, 'lon', 'lat', 'grp')
- tracers_out: float32 [12, 32, 128, 128], P(None, 'lat', ('grp', 'lon'))
The draws below stay inside these ranges and needn't reach their ends.
All inputs are finite; a program needn't handle non-finite values.
Results may differ from the reference program's by a relative error of at most 0.000052.
Values sent between devices are 32-bit elements; how exact they have to be, the bound alone decides.
A program may use at most 64 MiB of HBM per device.

```python
import math
import jax
import jax.numpy as jnp
from jax import lax

NF = 5
NT = 12
NR = 24
NH = 4
NX = 32
NY = 128
NZ = 128


def set_ends(values, rng, low, high):
    longest = values.shape.index(max(values.shape))
    spots = []
    for shift in (0, 1):
        where = [jax.random.randint(jax.random.fold_in(rng, axis), (), 0, length) for axis, length in enumerate(values.shape)]
        where[longest] = (where[longest] + shift) % values.shape[longest]
        spots.append(tuple(where))
    return values.at[spots[0]].set(low).at[spots[1]].set(high)


def level_of(own_key, extent, pieces, smallest, high):
    gain, own = 1.0, jax.random.fold_in(own_key, 6)
    for axis_at, blocks in pieces:
        draws = jnp.exp(jax.random.uniform(jax.random.fold_in(own, axis_at), (blocks,), jnp.float32, smallest / len(pieces), high / len(pieces)))
        gain = gain * jnp.repeat(draws, extent[axis_at] // blocks).reshape([-1 if axis == axis_at else 1 for axis in range(len(extent))])
    return gain


def gaussian(own_key, shape, spread, bound, shards=(), kind=jnp.bfloat16):
    array = spread * jax.random.normal(own_key, shape, jnp.float32)
    if shards:
        array = array * level_of(own_key, shape, shards, -0.22, 0.18)
    return jnp.clip(array, -bound, bound).astype(kind)


def setup_inputs(seed: int = 0) -> dict:
    keys = jax.random.split(jax.random.key(seed), 8)
    return {
        "state": gaussian(keys[0], (NF, NZ, NX, NY), 1.0, 5.0, ((1, 32),), jnp.float32),
        "tracers": jnp.clip(jnp.exp(math.log(1.5) - 2.7080502 * jax.random.uniform(keys[1], (NT, NX, NY, NZ), jnp.float32) ** level_of(keys[1], (NT, NX, NY, NZ), ((2, 32),), -0.2, 0.2)), 0.1, 1.5),
        "coupling": gaussian(keys[2], (NF, NF), 0.2, 0.8, (), jnp.float32),
        "rates": jnp.clip(jnp.exp(jax.random.uniform(keys[3], (NR,), jnp.float32, math.log(0.05), math.log(0.5))), 0.05, 0.5),
        "pairs": set_ends(jax.random.randint(keys[4], (NR, 3), 0, NT), jax.random.fold_in(keys[4], 1), 0, NT - 1).astype(jnp.int32),
        "heat_map": set_ends(jax.random.randint(keys[5], (NT,), 0, NH), jax.random.fold_in(keys[5], 1), 0, NH - 1).astype(jnp.int32),
        "heat_coef": jnp.clip(jax.random.uniform(keys[6], (NH,), jnp.float32, 0.5, 2.0), 0.5, 2.0),
    }


HIGH = lax.Precision.HIGHEST


def neighbour(field, offset, axis, periodic):
    if periodic:
        return jnp.roll(field, -offset, axis)
    length = field.shape[axis]
    zeros = jnp.zeros_like(lax.slice_in_dim(field, 0, abs(offset), axis=axis))
    if offset > 0:
        return jnp.concatenate([lax.slice_in_dim(field, offset, length, axis=axis), zeros], axis)
    return jnp.concatenate([zeros, lax.slice_in_dim(field, 0, length + offset, axis=axis)], axis)


def stencil(center, plus_one, plus_two, minus_one, minus_two):
    advect = -(8.0 * (plus_one - minus_one) - (plus_two - minus_two)) * (0.3 / 12.0)
    return advect + 0.1 * (plus_one + minus_one - 2.0 * center)


def tendency(fields, coupling):
    along_x = stencil(fields, neighbour(fields, 1, 2, False), neighbour(fields, 2, 2, False),
                      neighbour(fields, -1, 2, False), neighbour(fields, -2, 2, False))
    along_y = stencil(fields, neighbour(fields, 1, 3, True), neighbour(fields, 2, 3, True),
                      neighbour(fields, -1, 3, True), neighbour(fields, -2, 3, True))
    mixed = jnp.einsum("fg,gzxy->fzxy", coupling, fields, precision=HIGH)
    return along_x + along_y + mixed


def clamped(field, axis):
    length = field.shape[axis]
    higher = jnp.concatenate([lax.slice_in_dim(field, 1, length, axis=axis),
                              lax.slice_in_dim(field, length - 1, length, axis=axis)], axis)
    lower = jnp.concatenate([lax.slice_in_dim(field, 0, 1, axis=axis),
                             lax.slice_in_dim(field, 0, length - 1, axis=axis)], axis)
    return higher, lower


def mixing_of(east_diff, north_diff):
    shear = east_diff * east_diff + north_diff * north_diff
    return 0.2 * shear / (1.0 + shear)


def column_step(species, mixing_k, vertical, rates, pairs, heat_map, heat_coef):
    speed = 0.4 * vertical / (1.0 + jnp.abs(vertical))
    rising = jnp.maximum(speed, 0.0)
    sinking = jnp.minimum(speed, 0.0)
    higher, lower = clamped(species, 2)
    advect = -rising * (species - lower) - sinking * (higher - species)
    diffuse = mixing_k * (higher - 2.0 * species + lower)
    flat = species.reshape(species.shape[0], -1)
    labels = jnp.arange(species.shape[0], dtype=jnp.int32)
    first = (pairs[:, 0:1] == labels[None, :]).astype(jnp.float32)
    second = (pairs[:, 1:2] == labels[None, :]).astype(jnp.float32)
    product = (pairs[:, 2:3] == labels[None, :]).astype(jnp.float32)
    conc_a = jnp.dot(first, flat, precision=HIGH)
    conc_b = jnp.dot(second, flat, precision=HIGH)
    reaction = rates[:, None] * conc_a * conc_b
    stoich = product - first - second
    change = jnp.dot(stoich.T, reaction, precision=HIGH)
    classes = jnp.arange(heat_coef.shape[0], dtype=jnp.int32)
    weights = jnp.dot((heat_map[:, None] == classes[None, :]).astype(jnp.float32), heat_coef, precision=HIGH)
    heat = jnp.dot(weights, change, precision=HIGH)
    renewed = species + advect + diffuse + change.reshape(species.shape)
    return renewed, heat.reshape(mixing_k.shape)


def runge_kutta(state, coupling):
    section_one = state + tendency(state, coupling)
    section_two = 0.75 * state + 0.25 * (section_one + tendency(section_one, coupling))
    return state / 3.0 + (2.0 / 3.0) * (section_two + tendency(section_two, coupling))


def reference(state, tracers, coupling, rates, pairs, heat_map, heat_coef):
    stepped = runge_kutta(state, coupling)

    def one_row(items):
        species, winds = items
        winds = jnp.transpose(winds, (0, 2, 1))
        higher, lower = clamped(winds[0:2], 2)
        diffs = higher - lower
        mixing_k = mixing_of(diffs[0], diffs[1])
        return column_step(species, mixing_k, winds[2], rates, pairs, heat_map, heat_coef)

    new_rows, heat_rows = lax.map(one_row, (jnp.moveaxis(tracers, 1, 0), jnp.moveaxis(stepped[0:3], 2, 0)))
    tracers_out = jnp.moveaxis(new_rows, 0, 1)
    heat = jnp.transpose(heat_rows, (2, 0, 1))
    state_out = stepped.at[3].set(stepped[3] + 0.5 * heat)
    return state_out, tracers_out
```

```python
import functools

import jax
import jax.numpy as jnp
from jax import lax
from jax.experimental import pallas as pl
from jax.experimental.pallas import tpu as pltpu
from jax.sharding import PartitionSpec as P

HIGH = lax.Precision.HIGHEST


def extended(block, sides, width, periodic):
    for axis, dim in sides:
        count = lax.axis_size(axis)
        forward = [(i, i + 1) for i in range(count - 1)]
        if periodic:
            forward.append((count - 1, 0))
        backward = [(target, source) for source, target in forward]
        low = lax.ppermute(
            lax.slice_in_dim(block, block.shape[dim] - width, None, axis=dim), axis, forward
        )
        high = lax.ppermute(lax.slice_in_dim(block, 0, width, axis=dim), axis, backward)
        block = jnp.concatenate([low, block, high], axis=dim)
    return block


def stencil(center, plus_one, plus_two, minus_one, minus_two):
    advect = -(8.0 * (plus_one - minus_one) - (plus_two - minus_two)) * (0.3 / 12.0)
    return advect + 0.1 * (plus_one + minus_one - 2.0 * center)


def tendency(fields, coupling):
    padded_x = extended(fields, (("lat", 2),), 2, False)
    padded_y = extended(fields, (("grp", 3),), 2, True)
    along_x = stencil(
        fields, padded_x[:, :, 3:-1], padded_x[:, :, 4:], padded_x[:, :, 1:-3], padded_x[:, :, :-4]
    )
    along_y = stencil(
        fields,
        padded_y[:, :, :, 3:-1],
        padded_y[:, :, :, 4:],
        padded_y[:, :, :, 1:-3],
        padded_y[:, :, :, :-4],
    )
    mixed = jnp.einsum("fg,gzxy->fzxy", coupling, fields, precision=HIGH)
    return along_x + along_y + mixed


def runge_kutta(state, coupling):
    section_one = state + tendency(state, coupling)
    section_two = 0.75 * state + 0.25 * (section_one + tendency(section_one, coupling))
    return state / 3.0 + 2.0 / 3.0 * (section_two + tendency(section_two, coupling))


def local_tendency(planes, coupling_ref, pad_ref):
    rows, lanes = planes[0].shape
    for a, plane in enumerate(planes):
        pad_ref[a, 8 : 8 + rows, :] = plane
    result = []
    for a, plane in enumerate(planes):
        plus_one = pad_ref[a, 9 : 9 + rows, :] + pltpu.roll(plane, lanes - 1, 1)
        minus_one = pad_ref[a, 7 : 7 + rows, :] + pltpu.roll(plane, 1, 1)
        plus_two = pad_ref[a, 10 : 10 + rows, :] + pltpu.roll(plane, lanes - 2, 1)
        minus_two = pad_ref[a, 6 : 6 + rows, :] + pltpu.roll(plane, 2, 1)
        total = 0.3 * minus_one - 0.1 * plus_one + 0.025 * (plus_two - minus_two) - 0.4 * plane
        for b, other in enumerate(planes):
            total = total + coupling_ref[a, b] * other
        result.append(total)
    return result


def swap_blocks(blocks):
    blocks = list(blocks)
    rows, lanes = blocks[0].shape
    lane = lax.broadcasted_iota(jnp.int32, (rows, lanes), 1)
    step = 1
    while step < len(blocks):
        upper = (lane & step) != 0
        for i in range(len(blocks)):
            if i & step == 0:
                first, second = blocks[i], blocks[i + step]
                blocks[i] = jnp.where(upper, pltpu.roll(second, step, 1), first)
                blocks[i + step] = jnp.where(upper, second, pltpu.roll(first, lanes - step, 1))
        step *= 2
    return blocks


def turned(blocks):
    return jnp.transpose(jnp.concatenate(swap_blocks(blocks), axis=0))


def column_kernel(
    axis, n, local_steps,
    state_ref, tracers_ref, coupling_ref, rates_ref, pairs_ref, map_ref, coef_ref,
    state_out, tracers_out,
    pad_ref, react_ref, heat_ref, mix_ref, speed_ref, send_ref, recv_ref,
    send_sem, recv_sem, own_sem,
):
    me = lax.axis_index(axis)
    fields, depth, rows, lanes = state_ref.shape
    species, columns, levels = tracers_ref.shape
    reactions = rates_ref.shape[0]
    half = 2 * depth

    barrier = pltpu.get_barrier_semaphore()

    def greet(k, carry):
        pl.semaphore_signal(
            barrier, inc=1, device_id={axis: lax.rem(me + k, n)},
            device_id_type=pl.DeviceIdType.MESH,
        )
        return carry

    lax.fori_loop(1, n, greet, 0)

    chunk = 16
    warmth = []
    for r in range(reactions):
        a, b, p = pairs_ref[r, 0], pairs_ref[r, 1], pairs_ref[r, 2]
        warmth.append(coef_ref[map_ref[p]] - coef_ref[map_ref[a]] - coef_ref[map_ref[b]])

    def react(i, carry):
        at = pl.ds(pl.multiple_of(i * chunk, chunk), chunk)
        heat = jnp.zeros((chunk, levels), jnp.float32)
        for r in range(reactions):
            rate = rates_ref[r] * tracers_ref[pairs_ref[r, 0], at, :] * tracers_ref[pairs_ref[r, 1], at, :]
            react_ref[r, at, :] = rate
            heat = heat + warmth[r] * rate
        heat_ref[at, :] = heat
        return carry

    lax.fori_loop(0, columns // chunk, react, 0)

    if local_steps:
        pad_ref[...] = jnp.zeros_like(pad_ref)
        for z in range(depth):
            pad = pad_ref.at[z]
            base = [state_ref[a, z] for a in range(fields)]
            slope = local_tendency(base, coupling_ref, pad)
            one = [f + t for f, t in zip(base, slope)]
            slope = local_tendency(one, coupling_ref, pad)
            two = [0.75 * f + 0.25 * (s + t) for f, s, t in zip(base, one, slope)]
            slope = local_tendency(two, coupling_ref, pad)
            for a in range(fields):
                state_out[a, z] = base[a] * (1.0 / 3.0) + (2.0 / 3.0) * (two[a] + slope[a])
    else:
        state_out[...] = state_ref[...]

    heat_blocks = [heat_ref[pl.ds(y, rows, stride=depth), :] for y in range(depth)]
    winds = [turned([state_out[a, z] for z in range(depth)]) for a in range(3)]
    parts = winds + [turned(heat_blocks)]
    sub = lax.broadcasted_iota(jnp.int32, (n // 2, half, lanes), 1)
    low_rows = sub < depth
    for g in range(2):
        first = parts[2 * g].reshape(n // 2, half, lanes)
        second = parts[2 * g + 1].reshape(n // 2, half, lanes)
        send_ref[:, 0, g] = jnp.where(low_rows, first, pltpu.roll(second, depth, 1))
        send_ref[:, 1, g] = jnp.where(low_rows, pltpu.roll(first, depth, 1), second)

    pl.semaphore_wait(barrier, n - 1)
    own = pltpu.make_async_copy(send_ref.at[me // 2, lax.rem(me, 2)], recv_ref.at[me], own_sem)
    own.start()

    def give(k, carry):
        peer = lax.rem(me + k, n)
        pltpu.make_async_remote_copy(
            src_ref=send_ref.at[peer // 2, lax.rem(peer, 2)],
            dst_ref=recv_ref.at[me],
            send_sem=send_sem,
            recv_sem=recv_sem,
            device_id={axis: peer},
            device_id_type=pl.DeviceIdType.MESH,
        ).start()
        return carry

    lax.fori_loop(1, n, give, 0)

    def change(s, carry):
        total = jnp.zeros((columns, levels), jnp.float32)
        for r in range(reactions):
            a, b, p = pairs_ref[r, 0], pairs_ref[r, 1], pairs_ref[r, 2]
            sign = (p == s).astype(jnp.int32) - (a == s).astype(jnp.int32) - (b == s).astype(jnp.int32)
            total = total + sign.astype(jnp.float32) * react_ref[r]
        tracers_out[s] = tracers_ref[s] + total
        return carry

    lax.fori_loop(0, species, change, 0)

    own.wait()
    others = recv_ref.at[pl.ds(0, n - 1)]
    pltpu.make_async_copy(others, others, recv_sem).wait()

    pair = recv_ref[:, 0]
    at = lax.broadcasted_iota(jnp.int32, pair.shape, 1) & (depth - 1)
    beyond = jnp.concatenate([pltpu.roll(pair, depth - 1, 1)[1:], pair[n - 1 :]], axis=0)
    before = jnp.concatenate([pair[:1], pltpu.roll(pair, half - depth + 1, 1)[: n - 1]], axis=0)
    higher = jnp.where(at == depth - 1, beyond, pltpu.roll(pair, half - 1, 1))
    lower = jnp.where(at == 0, before, pltpu.roll(pair, 1, 1))
    square = (higher - lower) * (higher - lower)
    shear = square + pltpu.roll(square, depth, 1)
    mixing = 0.2 * shear / (1.0 + shear)
    mixing = mixing.reshape(n // 2, 2, half, lanes)
    mixing = jnp.where(low_rows, mixing[:, 0], mixing[:, 1]).reshape(levels, columns)
    other = recv_ref[:, 1].reshape(n // 2, 2, half, lanes)
    even, odd = other[:, 0], other[:, 1]
    vertical = jnp.where(low_rows, even, pltpu.roll(odd, depth, 1)).reshape(levels, columns)
    speed = 0.4 * vertical / (1.0 + jnp.abs(vertical))
    heated = jnp.where(low_rows, pltpu.roll(even, depth, 1), odd).reshape(n * depth, lanes)
    mixing, speed, heated = jnp.transpose(mixing), jnp.transpose(speed), jnp.transpose(heated)
    for z in range(depth):
        state_out[3, z] = state_out[3, z] + 0.5 * heated[z * rows : (z + 1) * rows]
    for y in range(depth):
        spread = pl.ds(y, rows, stride=depth)
        mix_ref[spread, :] = mixing[y * rows : (y + 1) * rows]
        speed_ref[spread, :] = speed[y * rows : (y + 1) * rows]
    level = lax.broadcasted_iota(jnp.int32, (columns, levels), 1)
    up = jnp.where(level == levels - 1, 0.0, mix_ref[...] - jnp.minimum(speed_ref[...], 0.0))
    down = jnp.where(level == 0, 0.0, mix_ref[...] + jnp.maximum(speed_ref[...], 0.0))
    mix_ref[...] = up
    speed_ref[...] = down

    def move(s, carry):
        conc = tracers_ref[s]
        below = conc - pltpu.roll(conc, 1, 1)
        above = pltpu.roll(below, levels - 1, 1)
        tracers_out[s] = tracers_out[s] + (mix_ref[...] * above - speed_ref[...] * below)
        return carry

    lax.fori_loop(0, species, move, 0)
    pltpu.make_async_copy(others, others, send_sem).wait()


def on_device(mesh, state, tracers, coupling, rates, pairs, heat_map, heat_coef):
    n = mesh.shape["lon"]
    local_steps = mesh.shape["lat"] == 1 and mesh.shape["grp"] == 1
    if not local_steps:
        state = runge_kutta(state, coupling)
    fields, depth, rows, lanes = state.shape
    species, levels = tracers.shape[0], tracers.shape[3]
    columns = tracers.shape[1] * tracers.shape[2]
    flat = tracers.reshape(species, columns, levels)
    vmem = pl.BlockSpec(memory_space=pltpu.VMEM)
    smem = pl.BlockSpec(memory_space=pltpu.SMEM)
    f32 = jnp.float32
    state_out, tracers_out = pl.pallas_call(
        functools.partial(column_kernel, "lon", n, local_steps),
        out_shape=(jax.ShapeDtypeStruct(state.shape, f32), jax.ShapeDtypeStruct(flat.shape, f32)),
        in_specs=[vmem] * 2 + [smem] * 5,
        out_specs=(vmem, vmem),
        scratch_shapes=[
            pltpu.VMEM((depth, fields, rows + 16, lanes), f32),
            pltpu.VMEM((rates.shape[0], columns, levels), f32),
            pltpu.VMEM((columns, levels), f32),
            pltpu.VMEM((columns, levels), f32),
            pltpu.VMEM((columns, levels), f32),
            pltpu.VMEM((n // 2, 2, 2, 2 * depth, lanes), f32),
            pltpu.VMEM((n, 2, 2 * depth, lanes), f32),
            pltpu.SemaphoreType.DMA,
            pltpu.SemaphoreType.DMA,
            pltpu.SemaphoreType.DMA,
        ],
        compiler_params=pltpu.CompilerParams(
            collective_id=0, has_side_effects=True, vmem_limit_bytes=32 * 2**20
        ),
    )(state, flat, coupling, rates, pairs, heat_map, heat_coef)
    return state_out, tracers_out.reshape(tracers.shape)


def solution(mesh):
    in_specs = (
        P(None, "lon", "lat", "grp"),
        P(None, "lat", ("grp", "lon"), None),
        P(),
        P(),
        P(),
        P(),
        P(),
    )
    out_specs = (P(None, "lon", "lat", "grp"), P(None, "lat", ("grp", "lon"), None))
    return jax.shard_map(
        functools.partial(on_device, mesh), mesh=mesh, in_specs=in_specs, out_specs=out_specs, check_vma=False
    )
```

```python
import functools

import jax
import jax.numpy as jnp
from jax import lax
from jax.experimental import pallas as pl
from jax.experimental.pallas import tpu as pltpu
from jax.sharding import PartitionSpec as P

HIGH = lax.Precision.HIGHEST


def extended(block, sides, width, periodic):
    for axis, dim in sides:
        count = lax.axis_size(axis)
        forward = [(i, i + 1) for i in range(count - 1)]
        if periodic:
            forward.append((count - 1, 0))
        backward = [(target, source) for source, target in forward]
        low = lax.ppermute(
            lax.slice_in_dim(block, block.shape[dim] - width, None, axis=dim), axis, forward
        )
        high = lax.ppermute(lax.slice_in_dim(block, 0, width, axis=dim), axis, backward)
        block = jnp.concatenate([low, block, high], axis=dim)
    return block


def stencil(center, plus_one, plus_two, minus_one, minus_two):
    advect = -(8.0 * (plus_one - minus_one) - (plus_two - minus_two)) * (0.3 / 12.0)
    return advect + 0.1 * (plus_one + minus_one - 2.0 * center)


def tendency(fields, coupling):
    padded_x = extended(fields, (("lat", 2),), 2, False)
    padded_y = extended(fields, (("grp", 3),), 2, True)
    along_x = stencil(
        fields, padded_x[:, :, 3:-1], padded_x[:, :, 4:], padded_x[:, :, 1:-3], padded_x[:, :, :-4]
    )
    along_y = stencil(
        fields,
        padded_y[:, :, :, 3:-1],
        padded_y[:, :, :, 4:],
        padded_y[:, :, :, 1:-3],
        padded_y[:, :, :, :-4],
    )
    mixed = jnp.einsum("fg,gzxy->fzxy", coupling, fields, precision=HIGH)
    return along_x + along_y + mixed


def runge_kutta(state, coupling):
    section_one = state + tendency(state, coupling)
    section_two = 0.75 * state + 0.25 * (section_one + tendency(section_one, coupling))
    return state / 3.0 + 2.0 / 3.0 * (section_two + tendency(section_two, coupling))


def local_tendency(planes, coupling_ref, pad_ref):
    rows, lanes = planes[0].shape
    for a, plane in enumerate(planes):
        pad_ref[a, 8 : 8 + rows, :] = plane
    result = []
    for a, plane in enumerate(planes):
        plus_one = pad_ref[a, 9 : 9 + rows, :] + pltpu.roll(plane, lanes - 1, 1)
        minus_one = pad_ref[a, 7 : 7 + rows, :] + pltpu.roll(plane, 1, 1)
        plus_two = pad_ref[a, 10 : 10 + rows, :] + pltpu.roll(plane, lanes - 2, 1)
        minus_two = pad_ref[a, 6 : 6 + rows, :] + pltpu.roll(plane, 2, 1)
        total = 0.3 * minus_one - 0.1 * plus_one + 0.025 * (plus_two - minus_two) - 0.4 * plane
        for b, other in enumerate(planes):
            total = total + coupling_ref[a, b] * other
        result.append(total)
    return result


def swap_blocks(blocks):
    blocks = list(blocks)
    rows, lanes = blocks[0].shape
    lane = lax.broadcasted_iota(jnp.int32, (rows, lanes), 1)
    step = 1
    while step < len(blocks):
        upper = (lane & step) != 0
        for i in range(len(blocks)):
            if i & step == 0:
                first, second = blocks[i], blocks[i + step]
                blocks[i] = jnp.where(upper, pltpu.roll(second, step, 1), first)
                blocks[i + step] = jnp.where(upper, second, pltpu.roll(first, lanes - step, 1))
        step *= 2
    return blocks


def paired(first, second, depth):
    half = 2 * depth
    first = first.reshape(-1, half, first.shape[-1])
    second = second.reshape(-1, half, second.shape[-1])
    low_rows = lax.broadcasted_iota(jnp.int32, first.shape, 1) < depth
    even = jnp.where(low_rows, first, pltpu.roll(second, depth, 1))
    odd = jnp.where(low_rows, pltpu.roll(first, depth, 1), second)
    return even, odd


def column_kernel(
    axis, n, local_steps,
    state_hbm, tracers_hbm, coupling_ref, rates_ref, pairs_ref, map_ref, coef_ref,
    state_out, tracers_out,
    state_ref, tracers_ref, pad_ref, react_ref, heat_ref, mix_ref, speed_ref, send_ref, recv_ref,
    load_sem, send_sem, recv_sem, own_sem,
):
    me = lax.axis_index(axis)
    fields, depth, rows, lanes = state_ref.shape
    species, columns, levels = tracers_ref.shape
    reactions = rates_ref.shape[0]
    groups = depth // 2

    loads = [
        pltpu.make_async_copy(
            state_hbm.at[:, pl.ds(2 * g, 2)], state_ref.at[:, pl.ds(2 * g, 2)], load_sem.at[g]
        )
        for g in range(groups)
    ]
    loads.append(pltpu.make_async_copy(tracers_hbm, tracers_ref, load_sem.at[groups]))
    for load in loads:
        load.start()

    barrier = pltpu.get_barrier_semaphore()

    def greet(k, carry):
        pl.semaphore_signal(
            barrier, inc=1, device_id={axis: lax.rem(me + k, n)},
            device_id_type=pl.DeviceIdType.MESH,
        )
        return carry

    lax.fori_loop(1, n, greet, 0)

    def weather(g):
        loads[g].wait()
        for z in (2 * g, 2 * g + 1):
            base = [state_ref[a, z] for a in range(fields)]
            if local_steps:
                pad = pad_ref.at[z]
                slope = local_tendency(base, coupling_ref, pad)
                one = [f + t for f, t in zip(base, slope)]
                slope = local_tendency(one, coupling_ref, pad)
                two = [0.75 * f + 0.25 * (s + t) for f, s, t in zip(base, one, slope)]
                slope = local_tendency(two, coupling_ref, pad)
                base = [f * (1.0 / 3.0) + (2.0 / 3.0) * (s + t) for f, s, t in zip(base, two, slope)]
            for a in range(fields):
                state_out[a, z] = base[a]

    def pack(g, heat):
        blocks = [
            jnp.transpose(jnp.concatenate([state_out[a, z] for a in range(3)] + [heat[z]], axis=0))
            for z in (2 * g, 2 * g + 1)
        ]
        even, odd = paired(blocks[0], blocks[1], depth)
        send_ref[g, :, 0] = even
        send_ref[g, :, 1] = odd

    def give(g):
        own = pltpu.make_async_copy(
            send_ref.at[g, me // 2, lax.rem(me, 2)], recv_ref.at[g, me], own_sem.at[g]
        )
        own.start()

        def one(k, carry):
            peer = lax.rem(me + k, n)
            pltpu.make_async_remote_copy(
                src_ref=send_ref.at[g, peer // 2, lax.rem(peer, 2)],
                dst_ref=recv_ref.at[g, me],
                send_sem=send_sem.at[g],
                recv_sem=recv_sem.at[g],
                device_id={axis: peer},
                device_id_type=pl.DeviceIdType.MESH,
            ).start()
            return carry

        lax.fori_loop(1, n, one, 0)
        return own

    pad_ref[:, :, 0:8, :] = jnp.zeros((depth, fields, 8, lanes), jnp.float32)
    pad_ref[:, :, 8 + rows :, :] = jnp.zeros((depth, fields, 8, lanes), jnp.float32)
    weather(0)

    warmth = []
    for r in range(reactions):
        a, b, p = pairs_ref[0, r], pairs_ref[1, r], pairs_ref[2, r]
        warmth.append(coef_ref[map_ref[p]] - coef_ref[map_ref[a]] - coef_ref[map_ref[b]])
    loads[groups].wait()
    chunk = 32

    def react(i, carry):
        at = pl.ds(pl.multiple_of(i * chunk, chunk), chunk)
        heat = jnp.zeros((chunk, levels), jnp.float32)
        for r in range(reactions):
            rate = rates_ref[r] * tracers_ref[pairs_ref[0, r], at, :] * tracers_ref[pairs_ref[1, r], at, :]
            react_ref[r, at, :] = rate
            heat = heat + warmth[r] * rate
        heat_ref[at, :] = heat
        return carry

    lax.fori_loop(0, columns // chunk, react, 0)
    heat = swap_blocks([heat_ref[pl.ds(y, rows, stride=depth), :] for y in range(depth)])

    owns = []
    for g in range(groups):
        if g:
            weather(g)
        pack(g, heat)
        if g == 0:
            pl.semaphore_wait(barrier, n - 1)
        owns.append(give(g))

    def change(s, carry):
        total = jnp.zeros((columns, levels), jnp.float32)
        for r in range(reactions):
            a, b, p = pairs_ref[0, r], pairs_ref[1, r], pairs_ref[2, r]
            sign = (p == s).astype(jnp.int32) - (a == s).astype(jnp.int32) - (b == s).astype(jnp.int32)
            total = total + sign.astype(jnp.float32) * react_ref[r]
        tracers_out[s] = tracers_ref[s] + total
        return carry

    lax.fori_loop(0, species, change, 0)

    others = recv_ref.at[0, pl.ds(0, n - 1)]
    winds = [[], [], []]
    for g in range(groups):
        owns[g].wait()
        pltpu.make_async_copy(others, others, recv_sem.at[g]).wait()
        tiles = recv_ref[g].reshape(n // 2, 2, 2 * depth, lanes)
        for z, block in zip((2 * g, 2 * g + 1), paired(tiles[:, 0], tiles[:, 1], depth)):
            block = jnp.transpose(block.reshape(n * depth, lanes))
            for a in range(3):
                winds[a].append(block[a * rows : (a + 1) * rows])
            state_out[3, z] = state_out[3, z] + 0.5 * block[3 * rows :]

    winds = [swap_blocks(blocks) for blocks in winds]
    level = lax.broadcasted_iota(jnp.int32, (rows, levels), 1)
    bottom, top = level == 0, level == levels - 1
    for y in range(depth):
        shear = jnp.zeros((rows, levels), jnp.float32)
        for wind in (winds[0][y], winds[1][y]):
            higher = jnp.where(top, wind, pltpu.roll(wind, levels - 1, 1))
            lower = jnp.where(bottom, wind, pltpu.roll(wind, 1, 1))
            shear = shear + (higher - lower) * (higher - lower)
        mixing = 0.2 * shear / (1.0 + shear)
        speed = 0.4 * winds[2][y] / (1.0 + jnp.abs(winds[2][y]))
        spread = pl.ds(y, rows, stride=depth)
        mix_ref[spread, :] = jnp.where(top, 0.0, mixing - jnp.minimum(speed, 0.0))
        speed_ref[spread, :] = jnp.where(bottom, 0.0, mixing + jnp.maximum(speed, 0.0))

    def move(s, carry):
        conc = tracers_ref[s]
        below = conc - pltpu.roll(conc, 1, 1)
        above = pltpu.roll(below, levels - 1, 1)
        tracers_out[s] = tracers_out[s] + (mix_ref[...] * above - speed_ref[...] * below)
        return carry

    lax.fori_loop(0, species, move, 0)
    for g in range(groups):
        pltpu.make_async_copy(others, others, send_sem.at[g]).wait()


def on_device(mesh, state, tracers, coupling, rates, pairs, heat_map, heat_coef):
    n = mesh.shape["lon"]
    local_steps = mesh.shape["lat"] == 1 and mesh.shape["grp"] == 1
    if not local_steps:
        state = runge_kutta(state, coupling)
    fields, depth, rows, lanes = state.shape
    species, levels = tracers.shape[0], tracers.shape[3]
    columns = tracers.shape[1] * tracers.shape[2]
    flat = tracers.reshape(species, columns, levels)
    vmem = pl.BlockSpec(memory_space=pltpu.VMEM)
    smem = pl.BlockSpec(memory_space=pltpu.SMEM)
    f32 = jnp.float32
    state_out, tracers_out = pl.pallas_call(
        functools.partial(column_kernel, "lon", n, local_steps),
        out_shape=(jax.ShapeDtypeStruct(state.shape, f32), jax.ShapeDtypeStruct(flat.shape, f32)),
        in_specs=[pl.BlockSpec(memory_space=pltpu.HBM)] * 2 + [smem] * 5,
        out_specs=(vmem, vmem),
        scratch_shapes=[
            pltpu.VMEM(state.shape, f32),
            pltpu.VMEM(flat.shape, f32),
            pltpu.VMEM((depth, fields, rows + 16, lanes), f32),
            pltpu.VMEM((rates.shape[0], columns, levels), f32),
            pltpu.VMEM((columns, levels), f32),
            pltpu.VMEM((columns, levels), f32),
            pltpu.VMEM((columns, levels), f32),
            pltpu.VMEM((depth // 2, n // 2, 2, 2 * depth, lanes), f32),
            pltpu.VMEM((depth // 2, n, 2 * depth, lanes), f32),
            pltpu.SemaphoreType.DMA((depth // 2 + 1,)),
            pltpu.SemaphoreType.DMA((depth // 2,)),
            pltpu.SemaphoreType.DMA((depth // 2,)),
            pltpu.SemaphoreType.DMA((depth // 2,)),
        ],
        compiler_params=pltpu.CompilerParams(
            collective_id=0, has_side_effects=True, vmem_limit_bytes=58 * 2**20
        ),
    )(state, flat, coupling, rates, pairs.T, heat_map, heat_coef)
    return state_out, tracers_out.reshape(tracers.shape)


def solution(mesh):
    in_specs = (
        P(None, "lon", "lat", "grp"),
        P(None, "lat", ("grp", "lon"), None),
        P(),
        P(),
        P(),
        P(),
        P(),
    )
    out_specs = (P(None, "lon", "lat", "grp"), P(None, "lat", ("grp", "lon"), None))
    return jax.shard_map(
        functools.partial(on_device, mesh), mesh=mesh, in_specs=in_specs, out_specs=out_specs, check_vma=False
    )
```

```python
import functools

import jax
import jax.numpy as jnp
from jax import lax
from jax.experimental import pallas as pl
from jax.experimental.pallas import tpu as pltpu
from jax.sharding import PartitionSpec as P

HIGH = lax.Precision.HIGHEST


def extended(block, sides, width, periodic):
    for axis, dim in sides:
        count = lax.axis_size(axis)
        forward = [(i, i + 1) for i in range(count - 1)]
        if periodic:
            forward.append((count - 1, 0))
        backward = [(target, source) for source, target in forward]
        low = lax.ppermute(
            lax.slice_in_dim(block, block.shape[dim] - width, None, axis=dim), axis, forward
        )
        high = lax.ppermute(lax.slice_in_dim(block, 0, width, axis=dim), axis, backward)
        block = jnp.concatenate([low, block, high], axis=dim)
    return block


def stencil(center, plus_one, plus_two, minus_one, minus_two):
    advect = -(8.0 * (plus_one - minus_one) - (plus_two - minus_two)) * (0.3 / 12.0)
    return advect + 0.1 * (plus_one + minus_one - 2.0 * center)


def tendency(fields, coupling):
    padded_x = extended(fields, (("lat", 2),), 2, False)
    padded_y = extended(fields, (("grp", 3),), 2, True)
    along_x = stencil(
        fields, padded_x[:, :, 3:-1], padded_x[:, :, 4:], padded_x[:, :, 1:-3], padded_x[:, :, :-4]
    )
    along_y = stencil(
        fields,
        padded_y[:, :, :, 3:-1],
        padded_y[:, :, :, 4:],
        padded_y[:, :, :, 1:-3],
        padded_y[:, :, :, :-4],
    )
    mixed = jnp.einsum("fg,gzxy->fzxy", coupling, fields, precision=HIGH)
    return along_x + along_y + mixed


def runge_kutta(state, coupling):
    section_one = state + tendency(state, coupling)
    section_two = 0.75 * state + 0.25 * (section_one + tendency(section_one, coupling))
    return state / 3.0 + 2.0 / 3.0 * (section_two + tendency(section_two, coupling))


def local_tendency(planes, coupling_ref, pad_ref):
    rows, lanes = planes[0].shape
    for a, plane in enumerate(planes):
        pad_ref[a, 8 : 8 + rows, :] = plane
    result = []
    for a, plane in enumerate(planes):
        plus_one = pad_ref[a, 9 : 9 + rows, :] + pltpu.roll(plane, lanes - 1, 1)
        minus_one = pad_ref[a, 7 : 7 + rows, :] + pltpu.roll(plane, 1, 1)
        plus_two = pad_ref[a, 10 : 10 + rows, :] + pltpu.roll(plane, lanes - 2, 1)
        minus_two = pad_ref[a, 6 : 6 + rows, :] + pltpu.roll(plane, 2, 1)
        total = 0.3 * minus_one - 0.1 * plus_one + 0.025 * (plus_two - minus_two) - 0.4 * plane
        for b, other in enumerate(planes):
            total = total + coupling_ref[a, b] * other
        result.append(total)
    return result


def swap_blocks(blocks):
    blocks = list(blocks)
    rows, lanes = blocks[0].shape
    lane = lax.broadcasted_iota(jnp.int32, (rows, lanes), 1)
    step = 1
    while step < len(blocks):
        upper = (lane & step) != 0
        for i in range(len(blocks)):
            if i & step == 0:
                first, second = blocks[i], blocks[i + step]
                blocks[i] = jnp.where(upper, pltpu.roll(second, step, 1), first)
                blocks[i + step] = jnp.where(upper, second, pltpu.roll(first, lanes - step, 1))
        step *= 2
    return blocks


def paired(first, second, depth):
    half = 2 * depth
    first = first.reshape(-1, half, first.shape[-1])
    second = second.reshape(-1, half, second.shape[-1])
    low_rows = lax.broadcasted_iota(jnp.int32, first.shape, 1) < depth
    even = jnp.where(low_rows, first, pltpu.roll(second, depth, 1))
    odd = jnp.where(low_rows, pltpu.roll(first, depth, 1), second)
    return even, odd


def column_kernel(
    axis, n, local_steps,
    state_ref, tracers_ref, coupling_ref, rates_ref, pairs_ref, map_ref, coef_ref,
    state_out, tracers_out, mix_ref, speed_ref,
    pad_ref, react_ref, heat_ref, send_ref, recv_ref,
    send_sem, recv_sem, own_sem,
):
    me = lax.axis_index(axis)
    fields, depth, rows, lanes = state_ref.shape
    species, columns, levels = tracers_ref.shape
    reactions = rates_ref.shape[0]
    groups = depth // 2

    barrier = pltpu.get_barrier_semaphore()

    def greet(k, carry):
        pl.semaphore_signal(
            barrier, inc=1, device_id={axis: lax.rem(me + k, n)},
            device_id_type=pl.DeviceIdType.MESH,
        )
        return carry

    lax.fori_loop(1, n, greet, 0)

    def weather(g):
        for z in (2 * g, 2 * g + 1):
            base = [state_ref[a, z] for a in range(fields)]
            if local_steps:
                pad = pad_ref.at[z]
                slope = local_tendency(base, coupling_ref, pad)
                one = [f + t for f, t in zip(base, slope)]
                slope = local_tendency(one, coupling_ref, pad)
                two = [0.75 * f + 0.25 * (s + t) for f, s, t in zip(base, one, slope)]
                slope = local_tendency(two, coupling_ref, pad)
                base = [f * (1.0 / 3.0) + (2.0 / 3.0) * (s + t) for f, s, t in zip(base, two, slope)]
            for a in range(fields):
                state_out[a, z] = base[a]

    def pack(g, heat):
        blocks = [
            jnp.transpose(jnp.concatenate([state_out[a, z] for a in range(3)] + [heat[z]], axis=0))
            for z in (2 * g, 2 * g + 1)
        ]
        even, odd = paired(blocks[0], blocks[1], depth)
        send_ref[g, :, 0] = even
        send_ref[g, :, 1] = odd

    def give(g):
        own = pltpu.make_async_copy(
            send_ref.at[g, me // 2, lax.rem(me, 2)], recv_ref.at[g, me], own_sem.at[g]
        )
        own.start()

        def one(k, carry):
            peer = lax.rem(me + k, n)
            pltpu.make_async_remote_copy(
                src_ref=send_ref.at[g, peer // 2, lax.rem(peer, 2)],
                dst_ref=recv_ref.at[g, me],
                send_sem=send_sem.at[g],
                recv_sem=recv_sem.at[g],
                device_id={axis: peer},
                device_id_type=pl.DeviceIdType.MESH,
            ).start()
            return carry

        lax.fori_loop(1, n, one, 0)
        return own

    pad_ref[:, :, 0:8, :] = jnp.zeros((depth, fields, 8, lanes), jnp.float32)
    pad_ref[:, :, 8 + rows :, :] = jnp.zeros((depth, fields, 8, lanes), jnp.float32)
    weather(0)

    warmth = []
    for r in range(reactions):
        a, b, p = pairs_ref[0, r], pairs_ref[1, r], pairs_ref[2, r]
        warmth.append(coef_ref[map_ref[p]] - coef_ref[map_ref[a]] - coef_ref[map_ref[b]])
    chunk = 32

    def react(i, carry):
        at = pl.ds(pl.multiple_of(i * chunk, chunk), chunk)
        heat = jnp.zeros((chunk, levels), jnp.float32)
        for r in range(reactions):
            rate = rates_ref[r] * tracers_ref[pairs_ref[0, r], at, :] * tracers_ref[pairs_ref[1, r], at, :]
            react_ref[r, at, :] = rate
            heat = heat + warmth[r] * rate
        heat_ref[at, :] = heat
        return carry

    lax.fori_loop(0, columns // chunk, react, 0)
    heat = swap_blocks([heat_ref[pl.ds(y, rows, stride=depth), :] for y in range(depth)])

    owns = []
    for g in range(groups):
        if g:
            weather(g)
        pack(g, heat)
        if g == 0:
            pl.semaphore_wait(barrier, n - 1)
        owns.append(give(g))

    def change(s, carry):
        total = jnp.zeros((columns, levels), jnp.float32)
        for r in range(reactions):
            a, b, p = pairs_ref[0, r], pairs_ref[1, r], pairs_ref[2, r]
            sign = (p == s).astype(jnp.int32) - (a == s).astype(jnp.int32) - (b == s).astype(jnp.int32)
            total = total + sign.astype(jnp.float32) * react_ref[r]
        tracers_out[s] = tracers_ref[s] + total
        return carry

    lax.fori_loop(0, species, change, 0)

    others = recv_ref.at[0, pl.ds(0, n - 1)]
    winds = [[], [], []]
    for g in range(groups):
        owns[g].wait()
        pltpu.make_async_copy(others, others, recv_sem.at[g]).wait()
        tiles = recv_ref[g].reshape(n // 2, 2, 2 * depth, lanes)
        for z, block in zip((2 * g, 2 * g + 1), paired(tiles[:, 0], tiles[:, 1], depth)):
            block = jnp.transpose(block.reshape(n * depth, lanes))
            for a in range(3):
                winds[a].append(block[a * rows : (a + 1) * rows])
            state_out[3, z] = state_out[3, z] + 0.5 * block[3 * rows :]

    winds = [swap_blocks(blocks) for blocks in winds]
    level = lax.broadcasted_iota(jnp.int32, (rows, levels), 1)
    bottom, top = level == 0, level == levels - 1
    for y in range(depth):
        shear = jnp.zeros((rows, levels), jnp.float32)
        for wind in (winds[0][y], winds[1][y]):
            higher = jnp.where(top, wind, pltpu.roll(wind, levels - 1, 1))
            lower = jnp.where(bottom, wind, pltpu.roll(wind, 1, 1))
            shear = shear + (higher - lower) * (higher - lower)
        mixing = 0.2 * shear / (1.0 + shear)
        speed = 0.4 * winds[2][y] / (1.0 + jnp.abs(winds[2][y]))
        spread = pl.ds(y, rows, stride=depth)
        mix_ref[spread, :] = jnp.where(top, 0.0, mixing - jnp.minimum(speed, 0.0))
        speed_ref[spread, :] = jnp.where(bottom, 0.0, mixing + jnp.maximum(speed, 0.0))

    for g in range(groups):
        pltpu.make_async_copy(others, others, send_sem.at[g]).wait()


def finish_kernel(
    state_ref, tracers_ref, changed_ref, mix_ref, speed_ref, state_out, tracers_out, moved_ref, sem
):
    species, columns, levels = tracers_ref.shape
    state_copy = pltpu.make_async_copy(state_ref, state_out, sem.at[species])
    state_copy.start()
    copies = []
    for s in range(species):
        conc = tracers_ref[s]
        below = conc - pltpu.roll(conc, 1, 1)
        above = pltpu.roll(below, levels - 1, 1)
        moved_ref[s] = changed_ref[s] + (mix_ref[...] * above - speed_ref[...] * below)
        copies.append(pltpu.make_async_copy(moved_ref.at[s], tracers_out.at[s], sem.at[s]))
        copies[-1].start()
    for copy in copies:
        copy.wait()
    state_copy.wait()


def on_device(mesh, state, tracers, coupling, rates, pairs, heat_map, heat_coef):
    n = mesh.shape["lon"]
    local_steps = mesh.shape["lat"] == 1 and mesh.shape["grp"] == 1
    if not local_steps:
        state = runge_kutta(state, coupling)
    fields, depth, rows, lanes = state.shape
    species, levels = tracers.shape[0], tracers.shape[3]
    columns = tracers.shape[1] * tracers.shape[2]
    flat = tracers.reshape(species, columns, levels)
    vmem = pl.BlockSpec(memory_space=pltpu.VMEM)
    smem = pl.BlockSpec(memory_space=pltpu.SMEM)
    hbm = pl.BlockSpec(memory_space=pltpu.HBM)
    f32 = jnp.float32
    whole_state = jax.ShapeDtypeStruct(state.shape, f32)
    whole_flat = jax.ShapeDtypeStruct(flat.shape, f32)
    plane = jax.ShapeDtypeStruct((columns, levels), f32)
    stepped, changed, mix, speed = pl.pallas_call(
        functools.partial(column_kernel, "lon", n, local_steps),
        out_shape=(whole_state, whole_flat, plane, plane),
        in_specs=[vmem] * 2 + [smem] * 5,
        out_specs=(vmem,) * 4,
        scratch_shapes=[
            pltpu.VMEM((depth, fields, rows + 16, lanes), f32),
            pltpu.VMEM((rates.shape[0], columns, levels), f32),
            pltpu.VMEM((columns, levels), f32),
            pltpu.VMEM((depth // 2, n // 2, 2, 2 * depth, lanes), f32),
            pltpu.VMEM((depth // 2, n, 2 * depth, lanes), f32),
            pltpu.SemaphoreType.DMA((depth // 2,)),
            pltpu.SemaphoreType.DMA((depth // 2,)),
            pltpu.SemaphoreType.DMA((depth // 2,)),
        ],
        compiler_params=pltpu.CompilerParams(
            collective_id=0, has_side_effects=True, vmem_limit_bytes=32 * 2**20
        ),
    )(state, flat, coupling, rates, pairs.T, heat_map, heat_coef)
    state_out, tracers_out = pl.pallas_call(
        finish_kernel,
        out_shape=(whole_state, whole_flat),
        in_specs=[vmem] * 5,
        out_specs=(hbm, hbm),
        scratch_shapes=[
            pltpu.VMEM(flat.shape, f32),
            pltpu.SemaphoreType.DMA((species + 1,)),
        ],
        compiler_params=pltpu.CompilerParams(vmem_limit_bytes=32 * 2**20),
    )(stepped, flat, changed, mix, speed)
    return state_out, tracers_out.reshape(tracers.shape)


def solution(mesh):
    in_specs = (
        P(None, "lon", "lat", "grp"),
        P(None, "lat", ("grp", "lon"), None),
        P(),
        P(),
        P(),
        P(),
        P(),
    )
    out_specs = (P(None, "lon", "lat", "grp"), P(None, "lat", ("grp", "lon"), None))
    return jax.shard_map(
        functools.partial(on_device, mesh), mesh=mesh, in_specs=in_specs, out_specs=out_specs, check_vma=False
    )
```

```python
import functools

import jax
import jax.numpy as jnp
from jax import lax
from jax.experimental import pallas as pl
from jax.experimental.pallas import tpu as pltpu
from jax.sharding import PartitionSpec as P

HIGH = lax.Precision.HIGHEST


def extended(block, sides, width, periodic):
    for axis, dim in sides:
        count = lax.axis_size(axis)
        forward = [(i, i + 1) for i in range(count - 1)]
        if periodic:
            forward.append((count - 1, 0))
        backward = [(target, source) for source, target in forward]
        low = lax.ppermute(
            lax.slice_in_dim(block, block.shape[dim] - width, None, axis=dim), axis, forward
        )
        high = lax.ppermute(lax.slice_in_dim(block, 0, width, axis=dim), axis, backward)
        block = jnp.concatenate([low, block, high], axis=dim)
    return block


def stencil(center, plus_one, plus_two, minus_one, minus_two):
    advect = -(8.0 * (plus_one - minus_one) - (plus_two - minus_two)) * (0.3 / 12.0)
    return advect + 0.1 * (plus_one + minus_one - 2.0 * center)


def tendency(fields, coupling):
    padded_x = extended(fields, (("lat", 2),), 2, False)
    padded_y = extended(fields, (("grp", 3),), 2, True)
    along_x = stencil(
        fields, padded_x[:, :, 3:-1], padded_x[:, :, 4:], padded_x[:, :, 1:-3], padded_x[:, :, :-4]
    )
    along_y = stencil(
        fields,
        padded_y[:, :, :, 3:-1],
        padded_y[:, :, :, 4:],
        padded_y[:, :, :, 1:-3],
        padded_y[:, :, :, :-4],
    )
    mixed = jnp.einsum("fg,gzxy->fzxy", coupling, fields, precision=HIGH)
    return along_x + along_y + mixed


def runge_kutta(state, coupling):
    section_one = state + tendency(state, coupling)
    section_two = 0.75 * state + 0.25 * (section_one + tendency(section_one, coupling))
    return state / 3.0 + 2.0 / 3.0 * (section_two + tendency(section_two, coupling))


def local_tendency(planes, coupling_ref, pad_ref):
    rows, lanes = planes[0].shape
    for a, plane in enumerate(planes):
        pad_ref[a, 8 : 8 + rows, :] = plane
    result = []
    for a, plane in enumerate(planes):
        plus_one = pad_ref[a, 9 : 9 + rows, :] + pltpu.roll(plane, lanes - 1, 1)
        minus_one = pad_ref[a, 7 : 7 + rows, :] + pltpu.roll(plane, 1, 1)
        plus_two = pad_ref[a, 10 : 10 + rows, :] + pltpu.roll(plane, lanes - 2, 1)
        minus_two = pad_ref[a, 6 : 6 + rows, :] + pltpu.roll(plane, 2, 1)
        total = 0.3 * minus_one - 0.1 * plus_one + 0.025 * (plus_two - minus_two) - 0.4 * plane
        for b, other in enumerate(planes):
            total = total + coupling_ref[a, b] * other
        result.append(total)
    return result


def step_kernel(state_ref, coupling_ref, stepped_ref, pad_ref):
    fields, depth, rows, lanes = state_ref.shape
    pad_ref[:, :, 0:8, :] = jnp.zeros((depth, fields, 8, lanes), jnp.float32)
    pad_ref[:, :, 8 + rows :, :] = jnp.zeros((depth, fields, 8, lanes), jnp.float32)
    for z in range(depth):
        pad = pad_ref.at[z]
        base = [state_ref[a, z] for a in range(fields)]
        slope = local_tendency(base, coupling_ref, pad)
        one = [f + t for f, t in zip(base, slope)]
        slope = local_tendency(one, coupling_ref, pad)
        two = [0.75 * f + 0.25 * (s + t) for f, s, t in zip(base, one, slope)]
        slope = local_tendency(two, coupling_ref, pad)
        for a in range(fields):
            stepped_ref[a, z] = base[a] * (1.0 / 3.0) + (2.0 / 3.0) * (two[a] + slope[a])


def swap_blocks(blocks):
    blocks = list(blocks)
    rows, lanes = blocks[0].shape
    lane = lax.broadcasted_iota(jnp.int32, (rows, lanes), 1)
    step = 1
    while step < len(blocks):
        upper = (lane & step) != 0
        for i in range(len(blocks)):
            if i & step == 0:
                first, second = blocks[i], blocks[i + step]
                blocks[i] = jnp.where(upper, pltpu.roll(second, step, 1), first)
                blocks[i + step] = jnp.where(upper, second, pltpu.roll(first, lanes - step, 1))
        step *= 2
    return blocks


def paired(first, second, depth):
    half = 2 * depth
    first = first.reshape(-1, half, first.shape[-1])
    second = second.reshape(-1, half, second.shape[-1])
    low_rows = lax.broadcasted_iota(jnp.int32, first.shape, 1) < depth
    even = jnp.where(low_rows, first, pltpu.roll(second, depth, 1))
    odd = jnp.where(low_rows, pltpu.roll(first, depth, 1), second)
    return even, odd


def column_kernel(
    axis, n,
    stepped_ref, tracers_ref, rates_ref, pairs_ref, map_ref, coef_ref,
    warm_ref, tracers_out, mix_ref, speed_ref,
    react_ref, heat_ref, send_ref, recv_ref,
    send_sem, recv_sem, own_sem,
):
    me = lax.axis_index(axis)
    depth, rows, lanes = warm_ref.shape
    species, columns, levels = tracers_ref.shape
    reactions = rates_ref.shape[0]
    groups = depth // 2

    barrier = pltpu.get_barrier_semaphore()

    def greet(k, carry):
        pl.semaphore_signal(
            barrier, inc=1, device_id={axis: lax.rem(me + k, n)},
            device_id_type=pl.DeviceIdType.MESH,
        )
        return carry

    lax.fori_loop(1, n, greet, 0)

    warmth = []
    for r in range(reactions):
        a, b, p = pairs_ref[0, r], pairs_ref[1, r], pairs_ref[2, r]
        warmth.append(coef_ref[map_ref[p]] - coef_ref[map_ref[a]] - coef_ref[map_ref[b]])
    chunk = 32

    def react(i, carry):
        at = pl.ds(pl.multiple_of(i * chunk, chunk), chunk)
        heat = jnp.zeros((chunk, levels), jnp.float32)
        for r in range(reactions):
            rate = rates_ref[r] * tracers_ref[pairs_ref[0, r], at, :] * tracers_ref[pairs_ref[1, r], at, :]
            react_ref[r, at, :] = rate
            heat = heat + warmth[r] * rate
        heat_ref[at, :] = heat
        return carry

    lax.fori_loop(0, columns // chunk, react, 0)
    heat = swap_blocks([heat_ref[pl.ds(y, rows, stride=depth), :] for y in range(depth)])

    for g in range(groups):
        blocks = [
            jnp.transpose(jnp.concatenate([stepped_ref[a, z] for a in range(3)] + [heat[z]], axis=0))
            for z in (2 * g, 2 * g + 1)
        ]
        even, odd = paired(blocks[0], blocks[1], depth)
        send_ref[:, 0, g] = even
        send_ref[:, 1, g] = odd

    pl.semaphore_wait(barrier, n - 1)

    def give(k, carry):
        peer = lax.rem(me + k, n)
        pltpu.make_async_remote_copy(
            src_ref=send_ref.at[peer // 2, lax.rem(peer, 2)],
            dst_ref=recv_ref.at[me],
            send_sem=send_sem,
            recv_sem=recv_sem,
            device_id={axis: peer},
            device_id_type=pl.DeviceIdType.MESH,
        ).start()
        return carry

    lax.fori_loop(1, n, give, 0)
    own = pltpu.make_async_copy(send_ref.at[me // 2, lax.rem(me, 2)], recv_ref.at[me], own_sem)
    own.start()

    def change(s, carry):
        total = jnp.zeros((columns, levels), jnp.float32)
        for r in range(reactions):
            a, b, p = pairs_ref[0, r], pairs_ref[1, r], pairs_ref[2, r]
            sign = (p == s).astype(jnp.int32) - (a == s).astype(jnp.int32) - (b == s).astype(jnp.int32)
            total = total + sign.astype(jnp.float32) * react_ref[r]
        tracers_out[s] = tracers_ref[s] + total
        return carry

    lax.fori_loop(0, species, change, 0)

    own.wait()
    others = recv_ref.at[pl.ds(0, n - 1)]
    pltpu.make_async_copy(others, others, recv_sem).wait()
    winds = [[], [], []]
    for g in range(groups):
        tiles = recv_ref[:, g].reshape(n // 2, 2, 2 * depth, lanes)
        for z, block in zip((2 * g, 2 * g + 1), paired(tiles[:, 0], tiles[:, 1], depth)):
            block = jnp.transpose(block.reshape(n * depth, lanes))
            for a in range(3):
                winds[a].append(block[a * rows : (a + 1) * rows])
            warm_ref[z] = stepped_ref[3, z] + 0.5 * block[3 * rows :]

    winds = [swap_blocks(blocks) for blocks in winds]
    level = lax.broadcasted_iota(jnp.int32, (rows, levels), 1)
    bottom, top = level == 0, level == levels - 1
    for y in range(depth):
        shear = jnp.zeros((rows, levels), jnp.float32)
        for wind in (winds[0][y], winds[1][y]):
            higher = jnp.where(top, wind, pltpu.roll(wind, levels - 1, 1))
            lower = jnp.where(bottom, wind, pltpu.roll(wind, 1, 1))
            shear = shear + (higher - lower) * (higher - lower)
        mixing = 0.2 * shear / (1.0 + shear)
        speed = 0.4 * winds[2][y] / (1.0 + jnp.abs(winds[2][y]))
        spread = pl.ds(y, rows, stride=depth)
        mix_ref[spread, :] = jnp.where(top, 0.0, mixing - jnp.minimum(speed, 0.0))
        speed_ref[spread, :] = jnp.where(bottom, 0.0, mixing + jnp.maximum(speed, 0.0))

    pltpu.make_async_copy(others, others, send_sem).wait()


def finish_kernel(
    stepped_ref, warm_ref, tracers_ref, changed_ref, mix_ref, speed_ref,
    state_out, tracers_out, moved_ref, sem,
):
    species, columns, levels = tracers_ref.shape
    copies = []
    for a in range(stepped_ref.shape[0]):
        source = warm_ref if a == 3 else stepped_ref.at[a]
        copies.append(pltpu.make_async_copy(source, state_out.at[a], sem.at[species + a]))
        copies[-1].start()
    for s in range(species):
        conc = tracers_ref[s]
        below = conc - pltpu.roll(conc, 1, 1)
        above = pltpu.roll(below, levels - 1, 1)
        moved_ref[s] = changed_ref[s] + (mix_ref[...] * above - speed_ref[...] * below)
        copies.append(pltpu.make_async_copy(moved_ref.at[s], tracers_out.at[s], sem.at[s]))
        copies[-1].start()
    for copy in copies:
        copy.wait()


def on_device(mesh, state, tracers, coupling, rates, pairs, heat_map, heat_coef):
    n = mesh.shape["lon"]
    fields, depth, rows, lanes = state.shape
    species, levels = tracers.shape[0], tracers.shape[3]
    columns = tracers.shape[1] * tracers.shape[2]
    flat = tracers.reshape(species, columns, levels)
    vmem = pl.BlockSpec(memory_space=pltpu.VMEM)
    smem = pl.BlockSpec(memory_space=pltpu.SMEM)
    hbm = pl.BlockSpec(memory_space=pltpu.HBM)
    f32 = jnp.float32
    whole_state = jax.ShapeDtypeStruct(state.shape, f32)
    whole_flat = jax.ShapeDtypeStruct(flat.shape, f32)
    plane = jax.ShapeDtypeStruct((columns, levels), f32)
    if mesh.shape["lat"] == 1 and mesh.shape["grp"] == 1:
        stepped = pl.pallas_call(
            step_kernel,
            out_shape=whole_state,
            in_specs=[vmem, smem],
            out_specs=vmem,
            scratch_shapes=[pltpu.VMEM((depth, fields, rows + 16, lanes), f32)],
            cost_estimate=pl.CostEstimate(
                flops=9000 * state.size, bytes_accessed=8 * state.size, transcendentals=0
            ),
            compiler_params=pltpu.CompilerParams(vmem_limit_bytes=32 * 2**20),
        )(state, coupling)
    else:
        stepped = runge_kutta(state, coupling)
    warm, changed, mix, speed = pl.pallas_call(
        functools.partial(column_kernel, "lon", n),
        out_shape=(jax.ShapeDtypeStruct(state.shape[1:], f32), whole_flat, plane, plane),
        in_specs=[vmem] * 2 + [smem] * 4,
        out_specs=(vmem,) * 4,
        scratch_shapes=[
            pltpu.VMEM((rates.shape[0], columns, levels), f32),
            pltpu.VMEM((columns, levels), f32),
            pltpu.VMEM((n // 2, 2, depth // 2, 2 * depth, lanes), f32),
            pltpu.VMEM((n, depth // 2, 2 * depth, lanes), f32),
            pltpu.SemaphoreType.DMA,
            pltpu.SemaphoreType.DMA,
            pltpu.SemaphoreType.DMA,
        ],
        compiler_params=pltpu.CompilerParams(
            collective_id=0, has_side_effects=True, vmem_limit_bytes=32 * 2**20
        ),
    )(stepped, flat, rates, pairs.T, heat_map, heat_coef)
    state_out, tracers_out = pl.pallas_call(
        finish_kernel,
        out_shape=(whole_state, whole_flat),
        in_specs=[vmem] * 6,
        out_specs=(hbm, hbm),
        scratch_shapes=[
            pltpu.VMEM(flat.shape, f32),
            pltpu.SemaphoreType.DMA((species + fields,)),
        ],
        compiler_params=pltpu.CompilerParams(vmem_limit_bytes=32 * 2**20),
    )(stepped, warm, flat, changed, mix, speed)
    return state_out, tracers_out.reshape(tracers.shape)


def solution(mesh):
    in_specs = (
        P(None, "lon", "lat", "grp"),
        P(None, "lat", ("grp", "lon"), None),
        P(),
        P(),
        P(),
        P(),
        P(),
    )
    out_specs = (P(None, "lon", "lat", "grp"), P(None, "lat", ("grp", "lon"), None))
    return jax.shard_map(
        functools.partial(on_device, mesh), mesh=mesh, in_specs=in_specs, out_specs=out_specs, check_vma=False
    )
```

```python
import functools

import jax
import jax.numpy as jnp
from jax import lax
from jax.experimental import pallas as pl
from jax.experimental.pallas import tpu as pltpu
from jax.sharding import PartitionSpec as P

HIGH = lax.Precision.HIGHEST


def extended(block, sides, width, periodic):
    for axis, dim in sides:
        count = lax.axis_size(axis)
        forward = [(i, i + 1) for i in range(count - 1)]
        if periodic:
            forward.append((count - 1, 0))
        backward = [(target, source) for source, target in forward]
        low = lax.ppermute(
            lax.slice_in_dim(block, block.shape[dim] - width, None, axis=dim), axis, forward
        )
        high = lax.ppermute(lax.slice_in_dim(block, 0, width, axis=dim), axis, backward)
        block = jnp.concatenate([low, block, high], axis=dim)
    return block


def stencil(center, plus_one, plus_two, minus_one, minus_two):
    advect = -(8.0 * (plus_one - minus_one) - (plus_two - minus_two)) * (0.3 / 12.0)
    return advect + 0.1 * (plus_one + minus_one - 2.0 * center)


def tendency(fields, coupling):
    padded_x = extended(fields, (("lat", 2),), 2, False)
    padded_y = extended(fields, (("grp", 3),), 2, True)
    along_x = stencil(
        fields, padded_x[:, :, 3:-1], padded_x[:, :, 4:], padded_x[:, :, 1:-3], padded_x[:, :, :-4]
    )
    along_y = stencil(
        fields,
        padded_y[:, :, :, 3:-1],
        padded_y[:, :, :, 4:],
        padded_y[:, :, :, 1:-3],
        padded_y[:, :, :, :-4],
    )
    mixed = jnp.einsum("fg,gzxy->fzxy", coupling, fields, precision=HIGH)
    return along_x + along_y + mixed


def runge_kutta(state, coupling):
    section_one = state + tendency(state, coupling)
    section_two = 0.75 * state + 0.25 * (section_one + tendency(section_one, coupling))
    return state / 3.0 + 2.0 / 3.0 * (section_two + tendency(section_two, coupling))


def local_tendency(planes, coupling_ref, pad_ref):
    rows, lanes = planes[0].shape
    for a, plane in enumerate(planes):
        pad_ref[a, 8 : 8 + rows, :] = plane
    result = []
    for a, plane in enumerate(planes):
        plus_one = pad_ref[a, 9 : 9 + rows, :] + pltpu.roll(plane, lanes - 1, 1)
        minus_one = pad_ref[a, 7 : 7 + rows, :] + pltpu.roll(plane, 1, 1)
        plus_two = pad_ref[a, 10 : 10 + rows, :] + pltpu.roll(plane, lanes - 2, 1)
        minus_two = pad_ref[a, 6 : 6 + rows, :] + pltpu.roll(plane, 2, 1)
        total = 0.3 * minus_one - 0.1 * plus_one + 0.025 * (plus_two - minus_two) - 0.4 * plane
        for b, other in enumerate(planes):
            total = total + coupling_ref[a, b] * other
        result.append(total)
    return result


def step_kernel(state_ref, coupling_ref, stepped_ref, pad_ref):
    fields, depth, rows, lanes = state_ref.shape
    pad_ref[:, :, 0:8, :] = jnp.zeros((depth, fields, 8, lanes), jnp.float32)
    pad_ref[:, :, 8 + rows :, :] = jnp.zeros((depth, fields, 8, lanes), jnp.float32)
    for z in range(depth):
        pad = pad_ref.at[z]
        base = [state_ref[a, z] for a in range(fields)]
        slope = local_tendency(base, coupling_ref, pad)
        one = [f + t for f, t in zip(base, slope)]
        slope = local_tendency(one, coupling_ref, pad)
        two = [0.75 * f + 0.25 * (s + t) for f, s, t in zip(base, one, slope)]
        slope = local_tendency(two, coupling_ref, pad)
        for a in range(fields):
            stepped_ref[a, z] = base[a] * (1.0 / 3.0) + (2.0 / 3.0) * (two[a] + slope[a])


def swap_blocks(blocks):
    blocks = list(blocks)
    rows, lanes = blocks[0].shape
    lane = lax.broadcasted_iota(jnp.int32, (rows, lanes), 1)
    step = 1
    while step < len(blocks):
        upper = (lane & step) != 0
        for i in range(len(blocks)):
            if i & step == 0:
                first, second = blocks[i], blocks[i + step]
                blocks[i] = jnp.where(upper, pltpu.roll(second, step, 1), first)
                blocks[i + step] = jnp.where(upper, second, pltpu.roll(first, lanes - step, 1))
        step *= 2
    return blocks


def paired(first, second, depth):
    half = 2 * depth
    first = first.reshape(-1, half, first.shape[-1])
    second = second.reshape(-1, half, second.shape[-1])
    low_rows = lax.broadcasted_iota(jnp.int32, first.shape, 1) < depth
    even = jnp.where(low_rows, first, pltpu.roll(second, depth, 1))
    odd = jnp.where(low_rows, pltpu.roll(first, depth, 1), second)
    return even, odd


def column_kernel(
    axis, n,
    stepped_ref, tracers_ref, rates_ref, pairs_ref, map_ref, coef_ref,
    warm_ref, tracers_out, mix_ref, speed_ref,
    react_ref, heat_ref, send_ref, recv_ref,
    send_sem, recv_sem, own_sem,
):
    me = lax.axis_index(axis)
    depth, rows, lanes = warm_ref.shape
    species, columns, levels = tracers_ref.shape
    reactions = rates_ref.shape[0]
    groups = depth // 2

    barrier = pltpu.get_barrier_semaphore()

    def greet(k, carry):
        pl.semaphore_signal(
            barrier, inc=1, device_id={axis: lax.rem(me + k, n)},
            device_id_type=pl.DeviceIdType.MESH,
        )
        return carry

    lax.fori_loop(1, n, greet, 0)

    warmth = []
    for r in range(reactions):
        a, b, p = pairs_ref[0, r], pairs_ref[1, r], pairs_ref[2, r]
        warmth.append(coef_ref[map_ref[p]] - coef_ref[map_ref[a]] - coef_ref[map_ref[b]])
    chunk = 32

    def react(i, carry):
        at = pl.ds(pl.multiple_of(i * chunk, chunk), chunk)
        heat = jnp.zeros((chunk, levels), jnp.float32)
        for r in range(reactions):
            rate = rates_ref[r] * tracers_ref[pairs_ref[0, r], at, :] * tracers_ref[pairs_ref[1, r], at, :]
            react_ref[r, at, :] = rate
            heat = heat + warmth[r] * rate
        heat_ref[at, :] = heat
        return carry

    lax.fori_loop(0, columns // chunk, react, 0)
    heat = swap_blocks([heat_ref[pl.ds(y, rows, stride=depth), :] for y in range(depth)])

    for g in range(groups):
        blocks = [
            jnp.transpose(jnp.concatenate([stepped_ref[a, z] for a in range(3)] + [heat[z]], axis=0))
            for z in (2 * g, 2 * g + 1)
        ]
        even, odd = paired(blocks[0], blocks[1], depth)
        send_ref[:, 0, g] = even
        send_ref[:, 1, g] = odd

    pl.semaphore_wait(barrier, n - 1)

    def give(j, carry):
        peer = lax.rem(me + 1 + lax.rem(j + n // 4 - 1, n - 1), n)
        pltpu.make_async_remote_copy(
            src_ref=send_ref.at[peer // 2, lax.rem(peer, 2)],
            dst_ref=recv_ref.at[me],
            send_sem=send_sem,
            recv_sem=recv_sem,
            device_id={axis: peer},
            device_id_type=pl.DeviceIdType.MESH,
        ).start()
        return carry

    lax.fori_loop(0, n - 1, give, 0)
    own = pltpu.make_async_copy(send_ref.at[me // 2, lax.rem(me, 2)], recv_ref.at[me], own_sem)
    own.start()

    def change(s, carry):
        total = jnp.zeros((columns, levels), jnp.float32)
        for r in range(reactions):
            a, b, p = pairs_ref[0, r], pairs_ref[1, r], pairs_ref[2, r]
            sign = (p == s).astype(jnp.int32) - (a == s).astype(jnp.int32) - (b == s).astype(jnp.int32)
            total = total + sign.astype(jnp.float32) * react_ref[r]
        tracers_out[s] = tracers_ref[s] + total
        return carry

    lax.fori_loop(0, species, change, 0)

    own.wait()
    others = recv_ref.at[pl.ds(0, n - 1)]
    pltpu.make_async_copy(others, others, recv_sem).wait()
    winds = [[], [], []]
    for g in range(groups):
        tiles = recv_ref[:, g].reshape(n // 2, 2, 2 * depth, lanes)
        for z, block in zip((2 * g, 2 * g + 1), paired(tiles[:, 0], tiles[:, 1], depth)):
            block = jnp.transpose(block.reshape(n * depth, lanes))
            for a in range(3):
                winds[a].append(block[a * rows : (a + 1) * rows])
            warm_ref[z] = stepped_ref[3, z] + 0.5 * block[3 * rows :]

    winds = [swap_blocks(blocks) for blocks in winds]
    level = lax.broadcasted_iota(jnp.int32, (rows, levels), 1)
    bottom, top = level == 0, level == levels - 1
    for y in range(depth):
        shear = jnp.zeros((rows, levels), jnp.float32)
        for wind in (winds[0][y], winds[1][y]):
            higher = jnp.where(top, wind, pltpu.roll(wind, levels - 1, 1))
            lower = jnp.where(bottom, wind, pltpu.roll(wind, 1, 1))
            shear = shear + (higher - lower) * (higher - lower)
        mixing = 0.2 * shear / (1.0 + shear)
        speed = 0.4 * winds[2][y] / (1.0 + jnp.abs(winds[2][y]))
        spread = pl.ds(y, rows, stride=depth)
        mix_ref[spread, :] = jnp.where(top, 0.0, mixing - jnp.minimum(speed, 0.0))
        speed_ref[spread, :] = jnp.where(bottom, 0.0, mixing + jnp.maximum(speed, 0.0))

    pltpu.make_async_copy(others, others, send_sem).wait()


def finish_kernel(
    stepped_ref, warm_ref, tracers_ref, changed_ref, mix_ref, speed_ref,
    state_out, tracers_out, moved_ref, sem,
):
    species, columns, levels = tracers_ref.shape
    copies = []
    for a in range(stepped_ref.shape[0]):
        source = warm_ref if a == 3 else stepped_ref.at[a]
        copies.append(pltpu.make_async_copy(source, state_out.at[a], sem.at[species + a]))
        copies[-1].start()
    for s in range(species):
        conc = tracers_ref[s]
        below = conc - pltpu.roll(conc, 1, 1)
        above = pltpu.roll(below, levels - 1, 1)
        moved_ref[s] = changed_ref[s] + (mix_ref[...] * above - speed_ref[...] * below)
        copies.append(pltpu.make_async_copy(moved_ref.at[s], tracers_out.at[s], sem.at[s]))
        copies[-1].start()
    for copy in copies:
        copy.wait()


def on_device(mesh, state, tracers, coupling, rates, pairs, heat_map, heat_coef):
    n = mesh.shape["lon"]
    fields, depth, rows, lanes = state.shape
    species, levels = tracers.shape[0], tracers.shape[3]
    columns = tracers.shape[1] * tracers.shape[2]
    flat = tracers.reshape(species, columns, levels)
    vmem = pl.BlockSpec(memory_space=pltpu.VMEM)
    smem = pl.BlockSpec(memory_space=pltpu.SMEM)
    hbm = pl.BlockSpec(memory_space=pltpu.HBM)
    f32 = jnp.float32
    whole_state = jax.ShapeDtypeStruct(state.shape, f32)
    whole_flat = jax.ShapeDtypeStruct(flat.shape, f32)
    plane = jax.ShapeDtypeStruct((columns, levels), f32)
    if mesh.shape["lat"] == 1 and mesh.shape["grp"] == 1:
        stepped = pl.pallas_call(
            step_kernel,
            out_shape=whole_state,
            in_specs=[vmem, smem],
            out_specs=vmem,
            scratch_shapes=[pltpu.VMEM((depth, fields, rows + 16, lanes), f32)],
            cost_estimate=pl.CostEstimate(
                flops=9000 * state.size, bytes_accessed=8 * state.size, transcendentals=0
            ),
            compiler_params=pltpu.CompilerParams(vmem_limit_bytes=32 * 2**20),
        )(state, coupling)
    else:
        stepped = runge_kutta(state, coupling)
    warm, changed, mix, speed = pl.pallas_call(
        functools.partial(column_kernel, "lon", n),
        out_shape=(jax.ShapeDtypeStruct(state.shape[1:], f32), whole_flat, plane, plane),
        in_specs=[vmem] * 2 + [smem] * 4,
        out_specs=(vmem,) * 4,
        scratch_shapes=[
            pltpu.VMEM((rates.shape[0], columns, levels), f32),
            pltpu.VMEM((columns, levels), f32),
            pltpu.VMEM((n // 2, 2, depth // 2, 2 * depth, lanes), f32),
            pltpu.VMEM((n, depth // 2, 2 * depth, lanes), f32),
            pltpu.SemaphoreType.DMA,
            pltpu.SemaphoreType.DMA,
            pltpu.SemaphoreType.DMA,
        ],
        compiler_params=pltpu.CompilerParams(
            collective_id=0, has_side_effects=True, vmem_limit_bytes=32 * 2**20
        ),
    )(stepped, flat, rates, pairs.T, heat_map, heat_coef)
    state_out, tracers_out = pl.pallas_call(
        finish_kernel,
        out_shape=(whole_state, whole_flat),
        in_specs=[vmem] * 6,
        out_specs=(hbm, hbm),
        scratch_shapes=[
            pltpu.VMEM(flat.shape, f32),
            pltpu.SemaphoreType.DMA((species + fields,)),
        ],
        compiler_params=pltpu.CompilerParams(vmem_limit_bytes=32 * 2**20),
    )(stepped, warm, flat, changed, mix, speed)
    return state_out, tracers_out.reshape(tracers.shape)


def solution(mesh):
    in_specs = (
        P(None, "lon", "lat", "grp"),
        P(None, "lat", ("grp", "lon"), None),
        P(),
        P(),
        P(),
        P(),
        P(),
    )
    out_specs = (P(None, "lon", "lat", "grp"), P(None, "lat", ("grp", "lon"), None))
    return jax.shard_map(
        functools.partial(on_device, mesh), mesh=mesh, in_specs=in_specs, out_specs=out_specs, check_vma=False
    )
```
